32 devices in a mesh: wide: 8 (over y, x, core), narrow: 4 (over z).
Axes of the slice: x: 2, y: 2, z: 4, core: 2. Of those that a mesh axis runs over, the one named last changes fastest.
Arguments:
- x_zero: bfloat16 [4608, 3456], P(('wide', 'narrow')), may hold values from -6 to 6
- labels: int32 [4608], P(('wide', 'narrow')), may hold values 0 or 1
- cross_u: bfloat16 [3456, 256], replicated, may hold values from -0.375 to 0.375
- cross_v: bfloat16 [3456, 256], replicated, may hold values from -0.109375 to 0.109375
- cross_bias: float32 [3456], replicated, may hold values from -3 to 3
- head: float32 [3456], replicated, may hold values from -0.109375 to 0.109375
- hot_table: float32 [8192, 128], replicated, may hold values from -6 to 6
- hot_acc: float32 [8192], replicated, may hold values from 0.01 to 100
- cold_table: float32 [65536, 128], P(('wide', 'narrow')), may hold values from -6 to 6
- cold_acc: float32 [65536], P(('wide', 'narrow')), may hold values from 0.0001 to 0.01
- hot_ids: int32 [4608, 26, 19], P(('wide', 'narrow')), may hold values from 0 to 8191
- cold_owner: int32 [4608, 26, 1], P(('wide', 'narrow')), may hold values from 0 to 31; in each aligned block of 3744 rows (0 to 3743, 3744 to 7487, ..., all dimensions but the last counted through in order) at most 468 rows name the same one
- cold_slot: int32 [4608, 26], P(('wide', 'narrow')), may hold values from 0 to 2047
Outputs:
- hot_out: float32 [8192, 128], replicated
- cold_out: float32 [65536, 128], P(('wide', 'narrow'))
- grad_u: bfloat16 [3456, 256], replicated
- grad_v: bfloat16 [3456, 256], replicated
- grad_bias: float32 [3456], replicated
The draws below stay inside these ranges and needn't reach their ends.
Inputs may be any that keep to these rules, and one draw needn't show every extreme that they name: `cold_owner`: an owner is a device's index over wide and narrow, wide slowest. Among the 3744 bags of one device no owner is named by more than 468 bags, a bound that some block reaches.
All inputs are finite; a program needn't handle non-finite values. No bound on the sum of `labels` on one device may be relied on, other than what follows from the above.
Results may differ from the reference program's by a relative error of at most 0.0058.
Values may be sent and summed in bfloat16 or wider, within the bound.
A program may use at most 128 MiB of HBM per device.

```python
import math
import jax
import jax.numpy as jnp
import numpy as np
from jax import lax

E = 128
F = 26
R = 256
HOT = 8192
B = 144
ROWS_DEV = 2048
HOT_PER = 19
D0 = 3456
TOTAL = 4608
ROWS = 65536
CAP = 468
N_WIDE = 8
N_NARROW = 4


def set_ends(result, own_key, smallest, largest):
    longest = result.shape.index(max(result.shape))
    spots = []
    for shift in (0, 1):
        where = [jax.random.randint(jax.random.fold_in(own_key, axis), (), 0, length) for axis, length in enumerate(result.shape)]
        where[longest] = (where[longest] + shift) % result.shape[longest]
        spots.append(tuple(where))
    return result.at[spots[0]].set(smallest).at[spots[1]].set(largest)


def block_levels(stream_key, extent, split, low, top_value):
    factor_of = 1.0
    for position, blocks in split:
        heights = jax.random.uniform(jax.random.fold_in(jax.random.fold_in(stream_key, 6), position), (blocks,), jnp.float32, low / len(split), top_value / len(split))
        factor_of = factor_of * jnp.repeat(jnp.exp(heights), extent[position] // blocks).reshape((-1,) + (1,) * (len(extent) - 1 - position))
    return factor_of


def rank_bounds(amount, slope):
    portions = [(1 << 20) // math.isqrt(standing ** slope) + 1 for standing in range(1, amount + 1)]
    width = 1 + sum(portions) // (1 << 30)
    return np.cumsum(np.array([max(1, weight // width) for weight in portions]))


def skewed_ids(stream_key, shape, number_of, slope):
    table = rank_bounds(number_of, slope)
    ticket = jax.random.randint(jax.random.fold_in(stream_key, 1), shape, 0, int(table[number_of - 1]))
    grade = jnp.searchsorted(jnp.asarray(table, jnp.int32), ticket, side="right")
    return jax.random.permutation(jax.random.fold_in(stream_key, 2), number_of)[grade].astype(jnp.int32)


def assign_block(rng, own, number, rows, number_of, top, limit, skew):
    order = jax.random.permutation(rng, number_of)
    packed, usual = shares(number_of, rows * top, limit, skew, True), shares(number_of, rows * top, limit, skew, False)
    places = jnp.arange(number_of)

    def named(lengths, offset_by):
        used = int((lengths > 0).sum())
        fixed = max(1, used // 4)
        passed = fixed + (places - fixed + offset_by * (used - fixed)) % max(1, number_of - fixed)
        return jnp.zeros((number_of,), jnp.int32).at[order[jnp.where(places < fixed, places, passed)]].set(jnp.asarray(lengths, jnp.int32))

    lengths = jnp.where(number % 4 == 0, named(packed, number // 4), named(usual, number - number // 4 - 1))
    mixed = jax.random.permutation(jax.random.fold_in(own, 3), number_of)
    donor, sink = mixed[0:number_of // 2 * 2:2], mixed[1:number_of // 2 * 2:2]
    margin = jnp.minimum(lengths[donor] - 1, limit - lengths[sink]) // 2
    margin = jnp.where((donor == order[0]) | (sink == order[0]) | (lengths[sink] == 0), 0, jnp.maximum(margin, 0))
    passed = jax.random.randint(jax.random.fold_in(own, 4), (number_of // 2,), 0, 1 << 20) % (margin + 1)
    lengths = lengths.at[donor].add(-passed).at[sink].add(passed)
    members = jnp.searchsorted(jnp.cumsum(lengths), jnp.arange(rows * top), side="right").astype(jnp.int32)
    grid = members.reshape(top, rows).T
    grid = grid[jax.random.permutation(jax.random.fold_in(own, 1), rows)]
    offset_by = jax.random.randint(jax.random.fold_in(own, 2), (rows, 1), 0, top)
    return jnp.take_along_axis(grid, (jnp.arange(top)[None, :] + offset_by) % top, axis=1)


def shares(amount, total, most, skew, full):
    weights = [(1 << 20) // math.isqrt(standing ** skew) + 1 for standing in range(1, amount + 1)]
    largest = most if full else min(most, max(-(-total // amount), total * weights[0] // sum(weights)))
    least = 1 if total - largest >= amount - 1 else 0
    holding, spare = [largest] + [least] * (amount - 1), total - largest - least * (amount - 1)
    while spare > 0:
        movable = [i for i in range(1, amount) if holding[i] < largest] or [i for i in range(1, amount) if holding[i] < most]
        whole, remaining = sum([weights[i] for i in movable]), spare
        for i in movable:
            addition = min(most - holding[i], max(1, remaining * weights[i] // whole), spare)
            holding[i] = holding[i] + addition
            spare = spare - addition
    return np.array(holding)


def gaussian(own_key, shape, width, reach, shards=(), held_as=jnp.bfloat16):
    values = jax.random.normal(own_key, shape, jnp.float32) * width
    if len(shards) > 0:
        values = block_levels(own_key, shape, shards, -0.22, 0.18) * values
    return jnp.clip(values, min=-reach, max=reach).astype(held_as)


def setup_inputs(seed: int = 0) -> dict:
    key_of = jax.random.split(jax.random.key(seed), 14)
    x_zero = gaussian(key_of[0], (TOTAL, D0), 1.0, 6.0, ((0, 32),))
    labels = set_ends((jax.random.randint(key_of[1], (TOTAL,), 0, 4) < 1).astype(jnp.int32), jax.random.fold_in(key_of[1], 1), 0, 1)
    cross_u = gaussian(key_of[2], (D0, R), R ** -0.5, 0.375)
    cross_v = gaussian(key_of[3], (D0, R), D0 ** -0.5, 0.109375)
    cross_bias = gaussian(key_of[4], (D0,), 0.5, 3.0, (), jnp.float32)
    head = gaussian(key_of[5], (D0,), D0 ** -0.5, 0.109375, (), jnp.float32)
    hot_table = gaussian(key_of[6], (HOT, E), 1.0, 6.0, (), jnp.float32)
    hot_acc = jnp.clip(jnp.exp(jax.random.uniform(key_of[7], (HOT,), jnp.float32, math.log(0.01), math.log(100.0))), 0.01, 100.0)
    cold_table = gaussian(key_of[8], (ROWS, E), 1.0, 6.0, ((0, 32),), jnp.float32)
    cold_acc = jnp.clip(jnp.exp(math.log(0.01) - 4.6051702 * jax.random.uniform(key_of[9], (ROWS,), jnp.float32) ** block_levels(key_of[9], (ROWS,), ((0, 32),), -0.2, 0.2)), 0.0001, 0.01)
    hot_ids = set_ends(skewed_ids(key_of[10], (TOTAL, F, HOT_PER), HOT, 2), jax.random.fold_in(key_of[10], 3), 0, HOT - 1).astype(jnp.int32)
    cold_owner_keys = jax.random.split(jax.random.fold_in(key_of[11], 1), TOTAL * F // (B * F))
    cold_owner_turns = jax.random.permutation(jax.random.fold_in(key_of[11], 3), TOTAL * F // (B * F))
    cold_owner = jax.vmap(lambda own, number: assign_block(jax.random.fold_in(key_of[11], 2), own, number, B * F, N_WIDE * N_NARROW, 1, CAP, 2))(cold_owner_keys, cold_owner_turns).reshape((TOTAL, F, 1))
    cold_slot = set_ends(jax.random.randint(key_of[12], (TOTAL, F), 0, ROWS_DEV), jax.random.fold_in(key_of[12], 1), 0, ROWS_DEV - 1).astype(jnp.int32)
    return {"x_zero": x_zero, "labels": labels, "cross_u": cross_u, "cross_v": cross_v, "cross_bias": cross_bias, "head": head, "hot_table": hot_table, "hot_acc": hot_acc, "cold_table": cold_table, "cold_acc": cold_acc, "hot_ids": hot_ids, "cold_owner": cold_owner, "cold_slot": cold_slot}


LEARN_RATE = 0.5
EPSILON = 1e-08

def backward_block(x_zero, labels, cross_u, cross_v, cross_bias, head):
    proj_b = jnp.dot(x_zero, cross_v, preferred_element_type=jnp.float32).astype(jnp.bfloat16)
    mixed = jnp.dot(proj_b, cross_u.T, preferred_element_type=jnp.float32)
    scale = mixed + cross_bias[None, :]
    x_float = x_zero.astype(jnp.float32)
    crossed = x_float * scale + x_float
    logit = lax.optimization_barrier(jnp.sum(crossed * head[None, :], axis=1))
    delta = jax.nn.sigmoid(logit) - labels.astype(jnp.float32)
    upstream = delta[:, None] * head[None, :]
    dscale = upstream * x_float
    dscale_b = dscale.astype(jnp.bfloat16)
    part_u = lax.dot_general(dscale_b, proj_b, (((0,), (0,)), ((), ())), preferred_element_type=jnp.float32)
    part_c = lax.optimization_barrier(jnp.sum(dscale, axis=0))
    dproj_b = jnp.dot(dscale_b, cross_u, preferred_element_type=jnp.float32).astype(jnp.bfloat16)
    part_v = lax.dot_general(x_zero, dproj_b, (((0,), (0,)), ((), ())), preferred_element_type=jnp.float32)
    pooled = upstream[:, E:] * (scale[:, E:] + 1.0) + jnp.dot(dproj_b, cross_v[E:].T, preferred_element_type=jnp.float32)
    return (part_u, part_v, part_c, pooled.astype(jnp.bfloat16))

def adagrad_rows(table, accum, grad):
    new_acc = accum + lax.optimization_barrier(jnp.mean(grad * grad, axis=1))
    return table - LEARN_RATE * grad / (jnp.sqrt(new_acc)[:, None] + EPSILON)

def reference(x_zero, labels, cross_u, cross_v, cross_bias, head, hot_table, hot_acc, cold_table, cold_acc, hot_ids, cold_owner, cold_slot):
    blocks = N_WIDE * N_NARROW

    def step(carry, item):
        hot_grad, cold_grad, sum_u, sum_v, sum_c = carry
        x_block, y_block, hot_block, owner_block, slot_block = item
        part_u, part_v, part_c, pooled = backward_block(x_block, y_block, cross_u, cross_v, cross_bias, head)
        flat_grad = pooled.reshape(B * F, E).astype(jnp.float32)
        hot_grad = hot_grad.at[hot_block.reshape(B * F, HOT_PER)].add(flat_grad[:, None, :])
        row_ids = (owner_block.reshape(B * F) * ROWS_DEV + slot_block.reshape(B * F)).astype(jnp.int32)
        cold_grad = cold_grad.at[row_ids].add(flat_grad)
        return ((hot_grad, cold_grad, sum_u + part_u, sum_v + part_v, sum_c + part_c), None)
    start = (jnp.zeros((HOT, E), jnp.float32), jnp.zeros((ROWS, E), jnp.float32), jnp.zeros((D0, R), jnp.float32), jnp.zeros((D0, R), jnp.float32), jnp.zeros((D0,), jnp.float32))
    items = (x_zero.reshape(blocks, B, D0), labels.reshape(blocks, B), hot_ids.reshape(blocks, B, F, HOT_PER), cold_owner.reshape(blocks, B, F), cold_slot.reshape(blocks, B, F))
    final, unused = lax.scan(step, start, items)
    hot_grad, cold_grad, sum_u, sum_v, sum_c = final
    hot_out = adagrad_rows(hot_table, hot_acc, hot_grad)
    cold_out = adagrad_rows(cold_table, cold_acc, cold_grad)
    return (hot_out, cold_out, sum_u.astype(jnp.bfloat16), sum_v.astype(jnp.bfloat16), sum_c)
```

```python
import functools

import jax
import jax.numpy as jnp
from jax import lax
from jax.experimental import pallas as pl
from jax.experimental.pallas import tpu as pltpu
from jax.sharding import PartitionSpec as P

LEARN_RATE = 0.5
EPSILON = 1e-08
AXES = ("wide", "narrow")
NT = (((1,), (1,)), ((), ()))
TN = (((0,), (0,)), ((), ()))
GROUP = 4
UNROLL = 8
COLD_WAYS = 4
HOT_WAYS = 8


def list_kernel(samples, features, stride, row_bits, shard_rows, owner_ref, slot_ref, me_ref, out_ref, count_ref):
    devices = count_ref.shape[0]

    @pl.loop(0, devices)
    def _(o):
        count_ref[o] = 0

    offset = me_ref[0] * samples

    @pl.loop(0, samples)
    def _(s):
        for f in range(features):
            b = s * features + f
            o = owner_ref[b]
            c = count_ref[o]
            out_ref[o * stride + c] = (slot_ref[b] << row_bits) + (offset + (f * GROUP * samples) + s)
            count_ref[o] = c + 1

    @pl.loop(0, devices)
    def _(o):
        c = count_ref[o]
        for i in range(UNROLL - 1):
            out_ref[o * stride + c + i] = shard_rows << row_bits
        out_ref[o * stride + (stride - 1)] = c


def hot_kernel(samples, features, lanes, ids_ref, g_ref, out_ref, *accs):
    rows, width = out_ref.shape
    step = 128

    @pl.loop(0, rows // step)
    def _(i):
        for acc in accs:
            acc[pl.ds(i * step, step), :] = jnp.zeros((step, width), jnp.float32)

    @pl.loop(0, samples)
    def _(s):
        @pl.loop(0, features, unroll=2)
        def _(f):
            row = g_ref[pl.ds(f * samples + s, 1), :]
            base = (s * features + f) * lanes
            for j in range(lanes):
                acc = accs[j % len(accs)]
                i = ids_ref[base + j]
                acc[pl.ds(i, 1), :] = acc[pl.ds(i, 1), :] + row

    @pl.loop(0, rows // step)
    def _(i):
        total = accs[0][pl.ds(i * step, step), :]
        for acc in accs[1:]:
            total = total + acc[pl.ds(i * step, step), :]
        out_ref[pl.ds(i * step, step), :] = total.astype(out_ref.dtype)


def cold_kernel(
    stride, row_bits, lists_ref, pd_ref, delta_ref, u_ref, v_ref, bias_ref, head_ref, table_ref, acc_ref, after_ref,
    out_ref, rows_ref, *accs
):
    step = pl.program_id(0)
    shard_rows, width = out_ref.shape
    rank = u_ref.shape[2]
    pairs, wide = u_ref.shape[0], u_ref.shape[1]
    block = pd_ref.shape[0]

    @pl.when(step == 0)
    def _():
        for acc in accs:
            acc[...] = jnp.zeros_like(acc)

    @pl.loop(0, pairs)
    def _(p):
        scale = lax.dot_general(pd_ref[:, :rank], u_ref[p], NT, preferred_element_type=jnp.float32) + bias_ref[p]
        back = lax.dot_general(pd_ref[:, rank:], v_ref[p], NT, preferred_element_type=jnp.float32)
        pooled = (delta_ref[...] * head_ref[p]) * (scale + 1.0) + back
        pooled = pooled.astype(jnp.bfloat16).astype(jnp.float32)
        for h in range(wide // width):
            first = pl.multiple_of((p * (wide // width) + h) * block, 8)
            rows_ref[pl.ds(first, block), :] = pooled[:, h * width:(h + 1) * width]

    for k in range(GROUP):
        count = lists_ref[0, 0, k * stride + (stride - 1)]

        @pl.loop(0, (count + (UNROLL - 1)) // UNROLL)
        def _(i):
            entries = [lists_ref[0, 0, k * stride + i * UNROLL + n] for n in range(UNROLL)]
            values = [rows_ref[pl.ds(e & ((1 << row_bits) - 1), 1), :] for e in entries]
            for n in range(UNROLL):
                acc = accs[n % len(accs)]
                slot = entries[n] >> row_bits
                acc[pl.ds(slot, 1), :] = acc[pl.ds(slot, 1), :] + values[n]

    @pl.when(step == pl.num_programs(0) - 1)
    def _():
        part = 256

        @pl.loop(0, shard_rows // part)
        def _(i):
            here = pl.ds(pl.multiple_of(i * part, part), part)
            grad = accs[0][here, :]
            for acc in accs[1:]:
                grad = grad + acc[here, :]
            new_acc = acc_ref[here, :] + jnp.mean(grad * grad, axis=1, keepdims=True)
            out_ref[here, :] = table_ref[here, :] - LEARN_RATE * grad / (jnp.sqrt(new_acc) + EPSILON)


def per_device(
    x_zero, labels, cross_u, cross_v, cross_bias, head, hot_table, hot_acc,
    cold_table, cold_acc, hot_ids, cold_owner, cold_slot,
):
    samples, depth = x_zero.shape
    shard_rows, width = cold_table.shape
    features, lanes = hot_ids.shape[1:]
    hot_rows = hot_table.shape[0]
    rank = cross_u.shape[1]
    bags = samples * features
    devices = lax.axis_size(AXES)
    capacity = 4 * bags // devices
    stride = -(-(capacity + UNROLL) // 128) * 128
    row_bits = (GROUP * bags - 1).bit_length()
    me = lax.axis_index(AXES)

    lists = pl.pallas_call(
        functools.partial(list_kernel, samples, features, stride, row_bits, shard_rows),
        out_shape=jax.ShapeDtypeStruct((devices * stride,), jnp.int32),
        in_specs=[pl.BlockSpec(memory_space=pltpu.SMEM)] * 3,
        out_specs=pl.BlockSpec(memory_space=pltpu.SMEM),
        scratch_shapes=[pltpu.SMEM((devices,), jnp.int32)],
        name="list_bags",
    )(cold_owner.reshape(bags), cold_slot.reshape(bags), lax.rem(me, GROUP).astype(jnp.int32).reshape(1))
    lists = lax.all_to_all(lists.reshape(devices, stride), AXES, split_axis=0, concat_axis=0, tiled=True)

    proj_b = jnp.dot(x_zero, cross_v, preferred_element_type=jnp.float32).astype(jnp.bfloat16)
    scale = lax.dot_general(proj_b, cross_u, NT, preferred_element_type=jnp.float32) + cross_bias[None, :]
    x_float = x_zero.astype(jnp.float32)
    crossed = x_float * scale + x_float
    logit = jnp.sum(crossed * head[None, :], axis=1)
    delta = jax.nn.sigmoid(logit) - labels.astype(jnp.float32)
    upstream = delta[:, None] * head[None, :]
    dscale = upstream * x_float
    dscale_b = dscale.astype(jnp.bfloat16)
    dproj_b = jnp.dot(dscale_b, cross_u, preferred_element_type=jnp.float32).astype(jnp.bfloat16)

    pd_all = lax.all_gather(jnp.concatenate([proj_b, dproj_b], axis=1), AXES, axis=0, tiled=True)
    delta_all = lax.all_gather(delta, AXES, axis=0, tiled=True)

    part_u = lax.dot_general(dscale_b, proj_b, TN, preferred_element_type=jnp.float32)
    part_v = lax.dot_general(x_zero, dproj_b, TN, preferred_element_type=jnp.float32)
    part_c = jnp.sum(dscale, axis=0)
    share = depth // devices
    flat_c = jnp.pad(part_c.reshape(devices, 1, share), ((0, 0), (0, 7), (0, rank - share)))
    flat_c, pd_all, delta_all = lax.optimization_barrier((flat_c, pd_all, delta_all))
    parts = jnp.concatenate(
        [part_u.reshape(devices, share, rank), part_v.reshape(devices, share, rank), flat_c], axis=1
    )
    sums = lax.psum_scatter(parts, AXES, scatter_dimension=0, tiled=True)[0]

    pooled = upstream[:, width:] * (scale[:, width:] + 1.0) + lax.dot_general(
        dproj_b, cross_v[width:], NT, preferred_element_type=jnp.float32
    )
    pooled = pooled.astype(jnp.bfloat16).astype(jnp.float32)
    grads = pooled.reshape(samples, features, width).transpose(1, 0, 2).reshape(bags, width)
    hot_part = pl.pallas_call(
        functools.partial(hot_kernel, samples, features, lanes),
        out_shape=jax.ShapeDtypeStruct((hot_rows, width), jnp.bfloat16),
        in_specs=[pl.BlockSpec(memory_space=pltpu.SMEM), pl.BlockSpec(memory_space=pltpu.VMEM)],
        out_specs=pl.BlockSpec(memory_space=pltpu.VMEM),
        scratch_shapes=[pltpu.VMEM((hot_rows, width), jnp.float32)] * HOT_WAYS,
        compiler_params=pltpu.CompilerParams(vmem_limit_bytes=48 << 20),
        cost_estimate=pl.CostEstimate(flops=80_000_000_000, bytes_accessed=8 << 20, transcendentals=0),
        name="hot_sum",
    )(hot_ids.reshape(bags * lanes), grads)
    hot_part, sums = lax.optimization_barrier((hot_part, sums))
    hot_share = lax.psum_scatter(hot_part, AXES, scatter_dimension=0, tiled=True)
    hot_grad = lax.all_gather(hot_share, AXES, axis=0, tiled=True)

    c_rows = sums[2 * share:]
    c_high = c_rows.astype(jnp.bfloat16)
    c_left = c_rows - c_high.astype(jnp.float32)
    c_mid = c_left.astype(jnp.bfloat16)
    c_low = (c_left - c_mid.astype(jnp.float32)).astype(jnp.bfloat16)
    c_sent = jnp.concatenate([c_high[:1], c_mid[:1], c_low[:1], jnp.zeros_like(c_high[:5])], axis=0)
    sent = jnp.concatenate([sums[:2 * share].astype(jnp.bfloat16), c_sent], axis=0)
    sent, hot_grad = lax.optimization_barrier((sent, hot_grad))
    hot_grad = hot_grad.astype(jnp.float32)
    both = lax.all_gather(sent, AXES, axis=0, tiled=False)
    grad_u = both[:, :share].reshape(depth, rank)
    grad_v = both[:, share:2 * share].reshape(depth, rank)
    c_back = both[:, 2 * share:2 * share + 3, :share].astype(jnp.float32)
    sum_c = ((c_back[:, 0] + c_back[:, 1]) + c_back[:, 2]).reshape(depth)

    pair = 2 if features % 2 == 0 else 1
    pairs, wide = features // pair, pair * width
    whole = lambda i: (0, 0)
    whole3 = lambda i: (0, 0, 0)
    block = GROUP * samples
    cold_out = pl.pallas_call(
        functools.partial(cold_kernel, stride, row_bits),
        grid=(devices // GROUP,),
        out_shape=jax.ShapeDtypeStruct(cold_table.shape, jnp.float32),
        in_specs=[
            pl.BlockSpec((1, 1, GROUP * stride), lambda i: (i, 0, 0), memory_space=pltpu.SMEM),
            pl.BlockSpec((block, 2 * rank), lambda i: (i, 0)),
            pl.BlockSpec((block, 1), lambda i: (i, 0)),
            pl.BlockSpec((pairs, wide, rank), whole3),
            pl.BlockSpec((pairs, wide, rank), whole3),
            pl.BlockSpec((pairs, 1, wide), whole3),
            pl.BlockSpec((pairs, 1, wide), whole3),
            pl.BlockSpec((shard_rows, width), whole),
            pl.BlockSpec((shard_rows, 1), whole),
            pl.BlockSpec(memory_space=pl.ANY),
        ],
        out_specs=pl.BlockSpec((shard_rows, width), whole),
        scratch_shapes=[pltpu.VMEM((features * block, width), jnp.float32)]
        + [pltpu.VMEM((shard_rows + 8, width), jnp.float32)] * COLD_WAYS,
        compiler_params=pltpu.CompilerParams(vmem_limit_bytes=48 << 20),
        cost_estimate=pl.CostEstimate(flops=50_000_000_000, bytes_accessed=16 << 20, transcendentals=0),
        name="cold_sum",
    )(
        lists.reshape(devices // GROUP, 1, GROUP * stride),
        pd_all,
        delta_all[:, None],
        cross_u[width:].reshape(pairs, wide, rank),
        cross_v[width:].reshape(pairs, wide, rank),
        cross_bias[width:].reshape(pairs, 1, wide),
        head[width:].reshape(pairs, 1, wide),
        cold_table,
        cold_acc[:, None],
        hot_part,
    )

    new_acc = hot_acc + jnp.mean(hot_grad * hot_grad, axis=1)
    hot_out = hot_table - LEARN_RATE * hot_grad / (jnp.sqrt(new_acc)[:, None] + EPSILON)
    return (hot_out, cold_out, grad_u, grad_v, sum_c)


def solution(mesh):
    rows = P(AXES)
    placed = (rows, rows, P(), P(), P(), P(), P(), P(), rows, rows, rows, rows, rows)
    return jax.shard_map(
        per_device,
        mesh=mesh,
        in_specs=placed,
        out_specs=(P(), rows, P(), P(), P()),
        check_vma=False,
    )
```

```python
import functools

import jax
import jax.numpy as jnp
from jax import lax
from jax.experimental import pallas as pl
from jax.experimental.pallas import tpu as pltpu
from jax.sharding import PartitionSpec as P

LEARN_RATE = 0.5
EPSILON = 1e-08
AXES = ("wide", "narrow")
NT = (((1,), (1,)), ((), ()))
TN = (((0,), (0,)), ((), ()))
GROUP = 4
UNROLL = 8
COLD_WAYS = 4
HOT_WAYS = 8


def list_kernel(samples, features, stride, row_bits, shard_rows, owner_ref, slot_ref, me_ref, out_ref, count_ref):
    devices = count_ref.shape[0]

    @pl.loop(0, devices)
    def _(o):
        count_ref[o] = 0

    offset = me_ref[0] * samples

    @pl.loop(0, samples)
    def _(s):
        for f in range(features):
            b = s * features + f
            o = owner_ref[b]
            c = count_ref[o]
            out_ref[o * stride + c] = (slot_ref[b] << row_bits) + (offset + (f * GROUP * samples) + s)
            count_ref[o] = c + 1

    @pl.loop(0, devices)
    def _(o):
        c = count_ref[o]
        for i in range(UNROLL - 1):
            out_ref[o * stride + c + i] = shard_rows << row_bits
        out_ref[o * stride + (stride - 1)] = c


def hot_kernel(samples, features, lanes, ids_ref, g_ref, after_ref, out_ref, *accs):
    rows, width = out_ref.shape
    step = 128

    @pl.loop(0, rows // step)
    def _(i):
        for acc in accs:
            acc[pl.ds(i * step, step), :] = jnp.zeros((step, width), jnp.float32)

    @pl.loop(0, samples)
    def _(s):
        @pl.loop(0, features, unroll=2)
        def _(f):
            row = g_ref[pl.ds(f * samples + s, 1), :]
            base = (s * features + f) * lanes
            for j in range(lanes):
                acc = accs[j % len(accs)]
                i = ids_ref[base + j]
                acc[pl.ds(i, 1), :] = acc[pl.ds(i, 1), :] + row

    @pl.loop(0, rows // step)
    def _(i):
        total = accs[0][pl.ds(i * step, step), :]
        for acc in accs[1:]:
            total = total + acc[pl.ds(i * step, step), :]
        out_ref[pl.ds(i * step, step), :] = total.astype(out_ref.dtype)


def cold_kernel(
    stride, row_bits, lists_ref, pd_ref, u_ref, v_ref, bias_ref, head_ref, table_ref, acc_ref, after_ref,
    out_ref, rows_ref, *accs
):
    step = pl.program_id(0)
    shard_rows, width = out_ref.shape
    rank = u_ref.shape[2]
    pairs, wide = u_ref.shape[0], u_ref.shape[1]
    block = pd_ref.shape[0]

    @pl.when(step == 0)
    def _():
        for acc in accs:
            acc[...] = jnp.zeros_like(acc)

    @pl.loop(0, pairs)
    def _(p):
        terms = pd_ref[:, 2 * rank:].astype(jnp.float32)
        delta = (terms[:, 0:1] + terms[:, 1:2]) + terms[:, 2:3]
        scale = lax.dot_general(pd_ref[:, :rank], u_ref[p], NT, preferred_element_type=jnp.float32) + bias_ref[p]
        back = lax.dot_general(pd_ref[:, rank:2 * rank], v_ref[p], NT, preferred_element_type=jnp.float32)
        pooled = (delta * head_ref[p]) * (scale + 1.0) + back
        pooled = pooled.astype(jnp.bfloat16).astype(jnp.float32)
        for h in range(wide // width):
            first = pl.multiple_of((p * (wide // width) + h) * block, 8)
            rows_ref[pl.ds(first, block), :] = pooled[:, h * width:(h + 1) * width]

    for k in range(GROUP):
        count = lists_ref[0, 0, k * stride + (stride - 1)]

        @pl.loop(0, (count + (UNROLL - 1)) // UNROLL)
        def _(i):
            entries = [lists_ref[0, 0, k * stride + i * UNROLL + n] for n in range(UNROLL)]
            values = [rows_ref[pl.ds(e & ((1 << row_bits) - 1), 1), :] for e in entries]
            for n in range(UNROLL):
                acc = accs[n % len(accs)]
                slot = entries[n] >> row_bits
                acc[pl.ds(slot, 1), :] = acc[pl.ds(slot, 1), :] + values[n]

    @pl.when(step == pl.num_programs(0) - 1)
    def _():
        part = 256

        @pl.loop(0, shard_rows // part)
        def _(i):
            here = pl.ds(pl.multiple_of(i * part, part), part)
            grad = accs[0][here, :]
            for acc in accs[1:]:
                grad = grad + acc[here, :]
            new_acc = acc_ref[here, :] + jnp.mean(grad * grad, axis=1, keepdims=True)
            out_ref[here, :] = table_ref[here, :] - LEARN_RATE * grad / (jnp.sqrt(new_acc) + EPSILON)


def sum_kernel(inner, outer, depth, *refs):
    count = len(refs) // 6
    takes, outs, half_in, halves, parts_in, parts = (refs[i * count:(i + 1) * count] for i in range(6))
    last_in = refs[6 * count:7 * count]
    send_sem, recv_sem = refs[7 * count:]
    w, n = lax.axis_index("wide"), lax.axis_index("narrow")
    a, b = lax.rem(w, inner), w // inner

    def peer(level, d):
        if level == 0:
            return {"wide": b * inner + lax.rem(a + d, inner)}, lax.rem(a + d, inner)
        if level == 1:
            return {"wide": lax.rem(b + d, outer) * inner + a}, lax.rem(b + d, outer)
        return {"narrow": lax.rem(n + d, depth)}, lax.rem(n + d, depth)

    sizes = (inner, outer, depth)
    barrier = pltpu.get_barrier_semaphore()
    for level in range(3):
        for d in range(1, sizes[level]):
            pl.semaphore_signal(barrier, inc=1, device_id=peer(level, d)[0], device_id_type=pl.DeviceIdType.MESH)
    pl.semaphore_wait(barrier, sum(sizes) - 3)

    index = [0]

    def send(src, dst, target):
        k = index[0]
        index[0] += 1
        copy = pltpu.make_async_remote_copy(
            src_ref=src, dst_ref=dst, send_sem=send_sem.at[k], recv_sem=recv_sem.at[k],
            device_id=target, device_id_type=pl.DeviceIdType.MESH,
        )
        copy.start()
        return copy

    def at(ref, part, rows):
        return ref.at[pl.ds(pl.multiple_of(part * rows, rows), rows)]

    def scatter(level, sources, slots, sums, own):
        copies = []
        for source, slot, total in zip(sources, slots, sums):
            rows = slot.shape[1]
            for d in range(1, sizes[level]):
                target, part = peer(level, d)
                copies.append(send(at(source, part, rows), slot.at[d - 1], target))
        for copy in copies:
            copy.wait()
        for source, slot, (total, base) in zip(sources, slots, sums):
            rows = slot.shape[1]
            step = 32 if rows % 32 == 0 else 16 if rows % 16 == 0 else 8

            @pl.loop(0, rows // step)
            def _(i):
                value = source[pl.ds(pl.multiple_of(own * rows + i * step, step), step), :].astype(jnp.float32)
                for d in range(1, sizes[level]):
                    value = value + slot[d - 1, pl.ds(pl.multiple_of(i * step, step), step), :].astype(jnp.float32)
                total[pl.ds(pl.multiple_of(base * rows + i * step, step), step), :] = value.astype(total.dtype)

    scatter(0, takes, half_in, [(t, 0) for t in halves], a)
    scatter(1, halves, parts_in, [(t, 0) for t in parts], b)
    scatter(2, parts, last_in, [(t, (a * outer + b) * depth + n) for t in outs], n)
    for level, place, share in ((2, (a * outer + b) * depth + n, inner * outer * depth), (1, a * outer + b, inner * outer), (0, a, inner)):
        copies = []
        for out in outs:
            rows = out.shape[0] // share
            for d in range(1, sizes[level]):
                copies.append(send(at(out, place, rows), at(out, place, rows), peer(level, d)[0]))
        for copy in copies:
            copy.wait()


def sum_all(arrays):
    wide, depth = lax.axis_size("wide"), lax.axis_size("narrow")
    inner = 2 if wide % 2 == 0 else 1
    outer = wide // inner
    shapes = lambda cut, slots=None: [
        pltpu.VMEM(((slots,) if slots else ()) + (x.shape[0] // cut,) + x.shape[1:], x.dtype) for x in arrays
    ]
    sends = 2 * len(arrays) * (inner + outer + depth - 3)
    return pl.pallas_call(
        functools.partial(sum_kernel, inner, outer, depth),
        out_shape=[jax.ShapeDtypeStruct(x.shape, x.dtype) for x in arrays],
        in_specs=[pl.BlockSpec(memory_space=pltpu.VMEM)] * len(arrays),
        out_specs=[pl.BlockSpec(memory_space=pltpu.VMEM)] * len(arrays),
        scratch_shapes=shapes(inner, max(inner - 1, 1)) + shapes(inner)
        + shapes(inner * outer, outer - 1) + shapes(inner * outer)
        + shapes(inner * outer * depth, depth - 1)
        + [pltpu.SemaphoreType.DMA((sends,)), pltpu.SemaphoreType.DMA((sends,))],
        compiler_params=pltpu.CompilerParams(collective_id=0, has_side_effects=True, vmem_limit_bytes=40 << 20),
        name="sum_all",
    )(*arrays)


def per_device(
    x_zero, labels, cross_u, cross_v, cross_bias, head, hot_table, hot_acc,
    cold_table, cold_acc, hot_ids, cold_owner, cold_slot,
):
    samples, depth = x_zero.shape
    shard_rows, width = cold_table.shape
    features, lanes = hot_ids.shape[1:]
    hot_rows = hot_table.shape[0]
    rank = cross_u.shape[1]
    bags = samples * features
    devices = lax.axis_size(AXES)
    capacity = 4 * bags // devices
    stride = -(-(capacity + UNROLL) // 128) * 128
    row_bits = (GROUP * bags - 1).bit_length()
    me = lax.axis_index(AXES)

    list_part = pl.pallas_call(
        functools.partial(list_kernel, samples, features, stride, row_bits, shard_rows),
        out_shape=jax.ShapeDtypeStruct((devices * stride,), jnp.int32),
        in_specs=[pl.BlockSpec(memory_space=pltpu.SMEM)] * 3,
        out_specs=pl.BlockSpec(memory_space=pltpu.SMEM),
        scratch_shapes=[pltpu.SMEM((devices,), jnp.int32)],
        name="list_bags",
    )(cold_owner.reshape(bags), cold_slot.reshape(bags), lax.rem(me, GROUP).astype(jnp.int32).reshape(1))
    lists = lax.all_to_all(list_part.reshape(devices, stride), AXES, split_axis=0, concat_axis=0, tiled=True)

    proj_b = jnp.dot(x_zero, cross_v, preferred_element_type=jnp.float32).astype(jnp.bfloat16)
    scale = lax.dot_general(proj_b, cross_u, NT, preferred_element_type=jnp.float32) + cross_bias[None, :]
    x_float = x_zero.astype(jnp.float32)
    crossed = x_float * scale + x_float
    logit = jnp.sum(crossed * head[None, :], axis=1)
    delta = jax.nn.sigmoid(logit) - labels.astype(jnp.float32)
    upstream = delta[:, None] * head[None, :]
    dscale = upstream * x_float
    dscale_b = dscale.astype(jnp.bfloat16)
    dproj_b = jnp.dot(dscale_b, cross_u, preferred_element_type=jnp.float32).astype(jnp.bfloat16)

    column = delta[:, None]
    high = column.astype(jnp.bfloat16)
    left = column - high.astype(jnp.float32)
    middle = left.astype(jnp.bfloat16)
    low = (left - middle.astype(jnp.float32)).astype(jnp.bfloat16)
    terms = jnp.pad(jnp.concatenate([high, middle, low], axis=1), ((0, 0), (0, width - 3)))
    pd_all = lax.all_gather(jnp.concatenate([proj_b, dproj_b, terms], axis=1), AXES, axis=0, tiled=True)

    part_u = lax.dot_general(dscale_b, proj_b, TN, preferred_element_type=jnp.float32)
    part_v = lax.dot_general(x_zero, dproj_b, TN, preferred_element_type=jnp.float32)
    part_c = jnp.sum(dscale, axis=0)
    unit = 16 * devices
    joined = jnp.concatenate([part_u.astype(jnp.bfloat16), part_v.astype(jnp.bfloat16)], axis=0)
    joined = jnp.pad(joined, ((0, -(2 * depth) % unit), (0, 0)))
    c_rows = jnp.pad(part_c.reshape(depth // width, width), ((0, -(depth // width) % (8 * devices)), (0, 0)))

    pooled = upstream[:, width:] * (scale[:, width:] + 1.0) + lax.dot_general(
        dproj_b, cross_v[width:], NT, preferred_element_type=jnp.float32
    )
    pooled = pooled.astype(jnp.bfloat16).astype(jnp.float32)
    grads = pooled.reshape(samples, features, width).transpose(1, 0, 2).reshape(bags, width)
    hot_part = pl.pallas_call(
        functools.partial(hot_kernel, samples, features, lanes),
        out_shape=jax.ShapeDtypeStruct((hot_rows, width), jnp.bfloat16),
        in_specs=[
            pl.BlockSpec(memory_space=pltpu.SMEM),
            pl.BlockSpec(memory_space=pltpu.VMEM),
            pl.BlockSpec(memory_space=pl.ANY),
        ],
        out_specs=pl.BlockSpec(memory_space=pltpu.VMEM),
        scratch_shapes=[pltpu.VMEM((hot_rows, width), jnp.float32)] * HOT_WAYS,
        compiler_params=pltpu.CompilerParams(vmem_limit_bytes=48 << 20),
        cost_estimate=pl.CostEstimate(flops=80_000_000_000, bytes_accessed=8 << 20, transcendentals=0),
        name="hot_sum",
    )(hot_ids.reshape(bags * lanes), grads, list_part)
    hot_grad, sum_uv, sum_rows = sum_all([hot_part, joined, c_rows])
    hot_grad = hot_grad.astype(jnp.float32)
    grad_u = sum_uv[:depth]
    grad_v = sum_uv[depth:2 * depth]
    sum_c = sum_rows[:depth // width].reshape(depth)

    pair = 2 if features % 2 == 0 else 1
    pairs, wide = features // pair, pair * width
    whole = lambda i: (0, 0)
    whole3 = lambda i: (0, 0, 0)
    block = GROUP * samples
    cold_out = pl.pallas_call(
        functools.partial(cold_kernel, stride, row_bits),
        grid=(devices // GROUP,),
        out_shape=jax.ShapeDtypeStruct(cold_table.shape, jnp.float32),
        in_specs=[
            pl.BlockSpec((1, 1, GROUP * stride), lambda i: (i, 0, 0), memory_space=pltpu.SMEM),
            pl.BlockSpec((block, 2 * rank + width), lambda i: (i, 0)),
            pl.BlockSpec((pairs, wide, rank), whole3),
            pl.BlockSpec((pairs, wide, rank), whole3),
            pl.BlockSpec((pairs, 1, wide), whole3),
            pl.BlockSpec((pairs, 1, wide), whole3),
            pl.BlockSpec((shard_rows, width), whole),
            pl.BlockSpec((shard_rows, 1), whole),
            pl.BlockSpec(memory_space=pl.ANY),
        ],
        out_specs=pl.BlockSpec((shard_rows, width), whole),
        scratch_shapes=[pltpu.VMEM((features * block, width), jnp.float32)]
        + [pltpu.VMEM((shard_rows + 8, width), jnp.float32)] * COLD_WAYS,
        compiler_params=pltpu.CompilerParams(vmem_limit_bytes=48 << 20),
        cost_estimate=pl.CostEstimate(flops=50_000_000_000, bytes_accessed=16 << 20, transcendentals=0),
        name="cold_sum",
    )(
        lists.reshape(devices // GROUP, 1, GROUP * stride),
        pd_all,
        cross_u[width:].reshape(pairs, wide, rank),
        cross_v[width:].reshape(pairs, wide, rank),
        cross_bias[width:].reshape(pairs, 1, wide),
        head[width:].reshape(pairs, 1, wide),
        cold_table,
        cold_acc[:, None],
        sum_c,
    )

    new_acc = hot_acc + jnp.mean(hot_grad * hot_grad, axis=1)
    hot_out = hot_table - LEARN_RATE * hot_grad / (jnp.sqrt(new_acc)[:, None] + EPSILON)
    return (hot_out, cold_out, grad_u, grad_v, sum_c)


def solution(mesh):
    rows = P(AXES)
    placed = (rows, rows, P(), P(), P(), P(), P(), P(), rows, rows, rows, rows, rows)
    return jax.shard_map(
        per_device,
        mesh=mesh,
        in_specs=placed,
        out_specs=(P(), rows, P(), P(), P()),
        check_vma=False,
    )
```

```python
import functools

import jax
import jax.numpy as jnp
from jax import lax
from jax.experimental import pallas as pl
from jax.experimental.pallas import tpu as pltpu
from jax.sharding import PartitionSpec as P

LEARN_RATE = 0.5
EPSILON = 1e-08
AXES = ("wide", "narrow")
NT = (((1,), (1,)), ((), ()))
TN = (((0,), (0,)), ((), ()))
GROUP = 4
UNROLL = 8
COLD_WAYS = 4
HOT_WAYS = 8


def list_kernel(samples, features, stride, row_bits, shard_rows, owner_ref, slot_ref, me_ref, out_ref, count_ref):
    devices = count_ref.shape[0]

    @pl.loop(0, devices)
    def _(o):
        count_ref[o] = 0

    offset = me_ref[0] * samples

    @pl.loop(0, samples)
    def _(s):
        for f in range(features):
            b = s * features + f
            o = owner_ref[b]
            c = count_ref[o]
            out_ref[o * stride + c] = (slot_ref[b] << row_bits) + (offset + (f * GROUP * samples) + s)
            count_ref[o] = c + 1

    @pl.loop(0, devices)
    def _(o):
        c = count_ref[o]
        for i in range(UNROLL - 1):
            out_ref[o * stride + c + i] = shard_rows << row_bits
        out_ref[o * stride + (stride - 1)] = c


def hot_kernel(samples, features, lanes, ids_ref, g_ref, after_ref, out_ref, *accs):
    rows, width = out_ref.shape
    step = 128

    @pl.loop(0, rows // step)
    def _(i):
        for acc in accs:
            acc[pl.ds(i * step, step), :] = jnp.zeros((step, width), jnp.float32)

    @pl.loop(0, samples)
    def _(s):
        @pl.loop(0, features, unroll=2)
        def _(f):
            row = g_ref[pl.ds(f * samples + s, 1), :]
            base = (s * features + f) * lanes
            for j in range(lanes):
                acc = accs[j % len(accs)]
                i = ids_ref[base + j]
                acc[pl.ds(i, 1), :] = acc[pl.ds(i, 1), :] + row

    @pl.loop(0, rows // step)
    def _(i):
        total = accs[0][pl.ds(i * step, step), :]
        for acc in accs[1:]:
            total = total + acc[pl.ds(i * step, step), :]
        out_ref[pl.ds(i * step, step), :] = total.astype(out_ref.dtype)


def cold_kernel(
    stride, row_bits, lists_ref, pd_ref, u_ref, v_ref, bias_ref, head_ref, table_ref, acc_ref, after_ref,
    out_ref, rows_ref, *accs
):
    step = pl.program_id(0)
    shard_rows, width = out_ref.shape
    rank = u_ref.shape[2]
    pairs, wide = u_ref.shape[0], u_ref.shape[1]
    block = pd_ref.shape[0]

    @pl.when(step == 0)
    def _():
        for acc in accs:
            acc[...] = jnp.zeros_like(acc)

    @pl.loop(0, pairs)
    def _(p):
        terms = pd_ref[:, 2 * rank:].astype(jnp.float32)
        delta = (terms[:, 0:1] + terms[:, 1:2]) + terms[:, 2:3]
        scale = lax.dot_general(pd_ref[:, :rank], u_ref[p], NT, preferred_element_type=jnp.float32) + bias_ref[p]
        back = lax.dot_general(pd_ref[:, rank:2 * rank], v_ref[p], NT, preferred_element_type=jnp.float32)
        pooled = (delta * head_ref[p]) * (scale + 1.0) + back
        pooled = pooled.astype(jnp.bfloat16).astype(jnp.float32)
        for h in range(wide // width):
            first = pl.multiple_of((p * (wide // width) + h) * block, 8)
            rows_ref[pl.ds(first, block), :] = pooled[:, h * width:(h + 1) * width]

    for k in range(GROUP):
        count = lists_ref[0, 0, k * stride + (stride - 1)]

        @pl.loop(0, (count + (UNROLL - 1)) // UNROLL)
        def _(i):
            entries = [lists_ref[0, 0, k * stride + i * UNROLL + n] for n in range(UNROLL)]
            values = [rows_ref[pl.ds(e & ((1 << row_bits) - 1), 1), :] for e in entries]
            for n in range(UNROLL):
                acc = accs[n % len(accs)]
                slot = entries[n] >> row_bits
                acc[pl.ds(slot, 1), :] = acc[pl.ds(slot, 1), :] + values[n]

    @pl.when(step == pl.num_programs(0) - 1)
    def _():
        part = 256

        @pl.loop(0, shard_rows // part)
        def _(i):
            here = pl.ds(pl.multiple_of(i * part, part), part)
            grad = accs[0][here, :]
            for acc in accs[1:]:
                grad = grad + acc[here, :]
            new_acc = acc_ref[here, :] + jnp.mean(grad * grad, axis=1, keepdims=True)
            out_ref[here, :] = table_ref[here, :] - LEARN_RATE * grad / (jnp.sqrt(new_acc) + EPSILON)


def sum_kernel(inner, outer, depth, *refs):
    count = (len(refs) - 2) // 7
    takes, outs, half_in, halves, parts_in, parts = (refs[i * count:(i + 1) * count] for i in range(6))
    last_in = refs[6 * count:7 * count]
    send_sem, recv_sem = refs[7 * count:]
    w, n = lax.axis_index("wide"), lax.axis_index("narrow")
    a, b = lax.rem(w, inner), w // inner

    def peer(level, d):
        if level == 0:
            return {"wide": b * inner + lax.rem(a + d, inner)}, lax.rem(a + d, inner)
        if level == 1:
            return {"wide": lax.rem(b + d, outer) * inner + a}, lax.rem(b + d, outer)
        return {"narrow": lax.rem(n + d, depth)}, lax.rem(n + d, depth)

    sizes = (inner, outer, depth)
    barrier = pltpu.get_barrier_semaphore()
    for level in range(3):
        for d in range(1, sizes[level]):
            pl.semaphore_signal(barrier, inc=1, device_id=peer(level, d)[0], device_id_type=pl.DeviceIdType.MESH)
    pl.semaphore_wait(barrier, sum(sizes) - 3)

    index = [0]

    def send(src, dst, target):
        k = index[0]
        index[0] += 1
        copy = pltpu.make_async_remote_copy(
            src_ref=src, dst_ref=dst, send_sem=send_sem.at[k], recv_sem=recv_sem.at[k],
            device_id=target, device_id_type=pl.DeviceIdType.MESH,
        )
        copy.start()
        return copy

    def at(ref, part, rows):
        return ref.at[pl.ds(pl.multiple_of(part * rows, rows), rows)]

    places = ((a * outer + b) * depth + n, a * outer + b, a)
    shares = (inner * outer * depth, inner * outer, inner)
    sources, slots, own = (takes, halves, parts), (half_in, parts_in, last_in), (a, b, n)
    totals, bases = (halves, parts, outs), (0, 0, places[0])

    def start(stage, i):
        copies = []
        if stage < 3:
            rows = slots[stage][i].shape[1]
            for d in range(1, sizes[stage]):
                target, part = peer(stage, d)
                copies.append(send(at(sources[stage][i], part, rows), slots[stage][i].at[d - 1], target))
        else:
            level = 5 - stage
            rows = outs[i].shape[0] // shares[stage - 3]
            block = at(outs[i], places[stage - 3], rows)
            for d in range(1, sizes[level]):
                copies.append(send(block, block, peer(level, d)[0]))
        return copies

    def add(level, i):
        source, slot, total = sources[level][i], slots[level][i], totals[level][i]
        rows = slot.shape[1]
        step = 32 if rows % 32 == 0 else 16 if rows % 16 == 0 else 8

        @pl.loop(0, rows // step)
        def _(r):
            value = source[pl.ds(pl.multiple_of(own[level] * rows + r * step, step), step), :].astype(jnp.float32)
            for d in range(1, sizes[level]):
                value = value + slot[d - 1, pl.ds(pl.multiple_of(r * step, step), step), :].astype(jnp.float32)
            total[pl.ds(pl.multiple_of(bases[level] * rows + r * step, step), step), :] = value.astype(total.dtype)

    flying = [start(0, i) for i in range(count)]
    for stage in range(6):
        for i in range(count):
            for copy in flying[i]:
                copy.wait()
            if stage < 3:
                add(stage, i)
            if stage < 5:
                flying[i] = start(stage + 1, i)


def sum_all(arrays):
    wide, depth = lax.axis_size("wide"), lax.axis_size("narrow")
    inner = 2 if wide % 2 == 0 else 1
    outer = wide // inner
    shapes = lambda cut, slots=None: [
        pltpu.VMEM(((slots,) if slots else ()) + (x.shape[0] // cut,) + x.shape[1:], x.dtype) for x in arrays
    ]
    sends = 2 * len(arrays) * (inner + outer + depth - 3)
    return pl.pallas_call(
        functools.partial(sum_kernel, inner, outer, depth),
        out_shape=[jax.ShapeDtypeStruct(x.shape, x.dtype) for x in arrays],
        in_specs=[pl.BlockSpec(memory_space=pltpu.VMEM)] * len(arrays),
        out_specs=[pl.BlockSpec(memory_space=pltpu.VMEM)] * len(arrays),
        scratch_shapes=shapes(inner, max(inner - 1, 1)) + shapes(inner)
        + shapes(inner * outer, outer - 1) + shapes(inner * outer)
        + shapes(inner * outer * depth, depth - 1)
        + [pltpu.SemaphoreType.DMA((sends,)), pltpu.SemaphoreType.DMA((sends,))],
        compiler_params=pltpu.CompilerParams(collective_id=0, has_side_effects=True, vmem_limit_bytes=40 << 20),
        name="sum_all",
    )(*arrays)


def per_device(
    x_zero, labels, cross_u, cross_v, cross_bias, head, hot_table, hot_acc,
    cold_table, cold_acc, hot_ids, cold_owner, cold_slot,
):
    samples, depth = x_zero.shape
    shard_rows, width = cold_table.shape
    features, lanes = hot_ids.shape[1:]
    hot_rows = hot_table.shape[0]
    rank = cross_u.shape[1]
    bags = samples * features
    devices = lax.axis_size(AXES)
    capacity = 4 * bags // devices
    stride = -(-(capacity + UNROLL) // 128) * 128
    row_bits = (GROUP * bags - 1).bit_length()
    me = lax.axis_index(AXES)

    list_part = pl.pallas_call(
        functools.partial(list_kernel, samples, features, stride, row_bits, shard_rows),
        out_shape=jax.ShapeDtypeStruct((devices * stride,), jnp.int32),
        in_specs=[pl.BlockSpec(memory_space=pltpu.SMEM)] * 3,
        out_specs=pl.BlockSpec(memory_space=pltpu.SMEM),
        scratch_shapes=[pltpu.SMEM((devices,), jnp.int32)],
        name="list_bags",
    )(cold_owner.reshape(bags), cold_slot.reshape(bags), lax.rem(me, GROUP).astype(jnp.int32).reshape(1))
    lists = lax.all_to_all(list_part.reshape(devices, stride), AXES, split_axis=0, concat_axis=0, tiled=True)

    proj_b = jnp.dot(x_zero, cross_v, preferred_element_type=jnp.float32).astype(jnp.bfloat16)
    scale = lax.dot_general(proj_b, cross_u, NT, preferred_element_type=jnp.float32) + cross_bias[None, :]
    x_float = x_zero.astype(jnp.float32)
    crossed = x_float * scale + x_float
    logit = jnp.sum(crossed * head[None, :], axis=1)
    delta = jax.nn.sigmoid(logit) - labels.astype(jnp.float32)
    upstream = delta[:, None] * head[None, :]
    dscale = upstream * x_float
    dscale_b = dscale.astype(jnp.bfloat16)
    dproj_b = jnp.dot(dscale_b, cross_u, preferred_element_type=jnp.float32).astype(jnp.bfloat16)

    column = delta[:, None]
    high = column.astype(jnp.bfloat16)
    left = column - high.astype(jnp.float32)
    middle = left.astype(jnp.bfloat16)
    low = (left - middle.astype(jnp.float32)).astype(jnp.bfloat16)
    terms = jnp.pad(jnp.concatenate([high, middle, low], axis=1), ((0, 0), (0, width - 3)))
    pd_all = lax.all_gather(jnp.concatenate([proj_b, dproj_b, terms], axis=1), AXES, axis=0, tiled=True)

    part_u = lax.dot_general(dscale_b, proj_b, TN, preferred_element_type=jnp.float32)
    part_v = lax.dot_general(x_zero, dproj_b, TN, preferred_element_type=jnp.float32)
    part_c = jnp.sum(dscale, axis=0)
    unit = 16 * devices
    sent_u = jnp.pad(part_u.astype(jnp.bfloat16), ((0, -depth % unit), (0, 0)))
    sent_v = jnp.pad(part_v.astype(jnp.bfloat16), ((0, -depth % unit), (0, 0)))
    c_rows = jnp.pad(part_c.reshape(depth // width, width), ((0, -(depth // width) % (8 * devices)), (0, 0)))

    pooled = upstream[:, width:] * (scale[:, width:] + 1.0) + lax.dot_general(
        dproj_b, cross_v[width:], NT, preferred_element_type=jnp.float32
    )
    pooled = pooled.astype(jnp.bfloat16).astype(jnp.float32)
    grads = pooled.reshape(samples, features, width).transpose(1, 0, 2).reshape(bags, width)
    hot_part = pl.pallas_call(
        functools.partial(hot_kernel, samples, features, lanes),
        out_shape=jax.ShapeDtypeStruct((hot_rows, width), jnp.bfloat16),
        in_specs=[
            pl.BlockSpec(memory_space=pltpu.SMEM),
            pl.BlockSpec(memory_space=pltpu.VMEM),
            pl.BlockSpec(memory_space=pl.ANY),
        ],
        out_specs=pl.BlockSpec(memory_space=pltpu.VMEM),
        scratch_shapes=[pltpu.VMEM((hot_rows, width), jnp.float32)] * HOT_WAYS,
        compiler_params=pltpu.CompilerParams(vmem_limit_bytes=48 << 20),
        cost_estimate=pl.CostEstimate(flops=80_000_000_000, bytes_accessed=8 << 20, transcendentals=0),
        name="hot_sum",
    )(hot_ids.reshape(bags * lanes), grads, list_part)
    hot_grad, sum_u, sum_v, sum_rows = sum_all([hot_part, sent_u, sent_v, c_rows])
    hot_grad = hot_grad.astype(jnp.float32)
    grad_u = sum_u[:depth]
    grad_v = sum_v[:depth]
    sum_c = sum_rows[:depth // width].reshape(depth)

    pair = 2 if features % 2 == 0 else 1
    pairs, wide = features // pair, pair * width
    whole = lambda i: (0, 0)
    whole3 = lambda i: (0, 0, 0)
    block = GROUP * samples
    cold_out = pl.pallas_call(
        functools.partial(cold_kernel, stride, row_bits),
        grid=(devices // GROUP,),
        out_shape=jax.ShapeDtypeStruct(cold_table.shape, jnp.float32),
        in_specs=[
            pl.BlockSpec((1, 1, GROUP * stride), lambda i: (i, 0, 0), memory_space=pltpu.SMEM),
            pl.BlockSpec((block, 2 * rank + width), lambda i: (i, 0)),
            pl.BlockSpec((pairs, wide, rank), whole3),
            pl.BlockSpec((pairs, wide, rank), whole3),
            pl.BlockSpec((pairs, 1, wide), whole3),
            pl.BlockSpec((pairs, 1, wide), whole3),
            pl.BlockSpec((shard_rows, width), whole),
            pl.BlockSpec((shard_rows, 1), whole),
            pl.BlockSpec(memory_space=pl.ANY),
        ],
        out_specs=pl.BlockSpec((shard_rows, width), whole),
        scratch_shapes=[pltpu.VMEM((features * block, width), jnp.float32)]
        + [pltpu.VMEM((shard_rows + 8, width), jnp.float32)] * COLD_WAYS,
        compiler_params=pltpu.CompilerParams(vmem_limit_bytes=48 << 20),
        cost_estimate=pl.CostEstimate(flops=50_000_000_000, bytes_accessed=16 << 20, transcendentals=0),
        name="cold_sum",
    )(
        lists.reshape(devices // GROUP, 1, GROUP * stride),
        pd_all,
        cross_u[width:].reshape(pairs, wide, rank),
        cross_v[width:].reshape(pairs, wide, rank),
        cross_bias[width:].reshape(pairs, 1, wide),
        head[width:].reshape(pairs, 1, wide),
        cold_table,
        cold_acc[:, None],
        sum_c,
    )

    new_acc = hot_acc + jnp.mean(hot_grad * hot_grad, axis=1)
    hot_out = hot_table - LEARN_RATE * hot_grad / (jnp.sqrt(new_acc)[:, None] + EPSILON)
    return (hot_out, cold_out, grad_u, grad_v, sum_c)


def solution(mesh):
    rows = P(AXES)
    placed = (rows, rows, P(), P(), P(), P(), P(), P(), rows, rows, rows, rows, rows)
    return jax.shard_map(
        per_device,
        mesh=mesh,
        in_specs=placed,
        out_specs=(P(), rows, P(), P(), P()),
        check_vma=False,
    )
```
